32 devices in a mesh: groups: 2 (over x), space: 16 (over z, y, core).
Axes of the slice: x: 2, y: 2, z: 4, core: 2. Of those that a mesh axis runs over, the one named last changes fastest.
Arguments:
- slide_map: float32 [256, 416, 128], P(('groups', 'space')), parts along dimension 0
- kernels: float32 [8, 3, 3, 416], replicated, may hold values from -2 to 2
- pointwise: float32 [8, 416, 416], replicated, may hold values from -0.3125 to 0.3125
- biases: float32 [8, 416], replicated, may hold values from -3 to 3
- classifier: float32 [416, 2], replicated, may hold values from -0.3125 to 0.3125
Outputs:
- features: float32 [256, 416, 128], P(('groups', 'space')), parts along dimension 0
- logits: float32 [4], P('groups'), parts along dimension 0
The draws below stay inside these ranges and needn't reach their ends.
There are 2 independent parts, one for each index of `groups`. The reference program is written for one: setup_inputs(seed, part) draws one part's arguments, and reference() takes and returns one part's arrays. A program takes and returns all parts, laid end to end along the dimension named above; an argument that names none is the same for every part. Nothing has to cross between parts.
All inputs are finite; a program needn't handle non-finite values.
Results may differ from the reference program's by a relative error of at most 0.00021.
Values sent between devices are 32-bit elements; how exact they have to be, the bound alone decides.
No kernel may reach another device: no remote copies, remote signals or barrier semaphores. Data moves between devices by JAX's collectives and lax.ppermute only.
A program may use at most 64 MiB of HBM per device.

```python
import jax
import jax.numpy as jnp
from jax import lax

CHANNELS = 416
COLUMNS = 128
CLASSES = 2
LAYERS = 8
HEIGHT = 128


def draw_slide_map(key, part):
    rising = 1.0 + 2.0 * jnp.arange(HEIGHT, dtype=jnp.float32) / (HEIGHT - 1)
    values = jax.random.normal(key, (HEIGHT, CHANNELS, COLUMNS), jnp.float32)
    return (values * rising[:, None, None]).astype(jnp.float32)


def gaussian(rng, dims, spread, reach, held_as=jnp.bfloat16):
    values = jax.random.normal(rng, dims, jnp.float32) * spread
    return jnp.minimum(jnp.maximum(values, -reach), reach).astype(held_as)


def setup_inputs(seed: int = 0, part: int = 0) -> dict:
    key_list = jax.random.split(jax.random.key(seed), 6)
    own_keys = jax.random.split(jax.random.fold_in(key_list[5], part), 6)
    slide_map = draw_slide_map(jax.random.fold_in(jax.random.fold_in(key_list[5], part), 71), part)
    kernels = gaussian(key_list[1], (LAYERS, 3, 3, CHANNELS), 9 ** -0.5, 2.0, jnp.float32)
    pointwise = gaussian(key_list[2], (LAYERS, CHANNELS, CHANNELS), CHANNELS ** -0.5, 0.3125, jnp.float32)
    biases = gaussian(key_list[3], (LAYERS, CHANNELS), 0.5, 3.0, jnp.float32)
    classifier = gaussian(key_list[4], (CHANNELS, CLASSES), CHANNELS ** -0.5, 0.3125, jnp.float32)
    return dict(slide_map=slide_map, kernels=kernels, pointwise=pointwise, biases=biases, classifier=classifier)


def apply_block(extended, kernel_set, mixing, shift):
    inner_rows = extended.shape[0] - 2
    width = extended.shape[2]
    activated = jnp.maximum(extended, 0.0)
    padded = jnp.pad(activated, ((0, 0), (0, 0), (1, 1)))
    spatial = jnp.zeros((inner_rows, extended.shape[1], width), jnp.float32)
    for row_offset in range(3):
        for col_offset in range(3):
            spatial = spatial + kernel_set[row_offset, col_offset][None, :, None] * padded[row_offset:row_offset + inner_rows, :, col_offset:col_offset + width]
    mixed = jnp.einsum("oc,rcw->row", mixing, spatial, precision=lax.Precision.HIGHEST)
    return extended[1:-1] + mixed + shift[None, :, None]


def reference(slide_map, kernels, pointwise, biases, classifier):
    features = slide_map
    for layer_index in range(LAYERS):
        extended = jnp.pad(features, ((1, 1), (0, 0), (0, 0)))
        features = apply_block(extended, kernels[layer_index], pointwise[layer_index], biases[layer_index])
    pooled = jnp.sum(features, axis=(0, 2)) / (HEIGHT * COLUMNS)
    logits = jnp.dot(pooled, classifier, precision=lax.Precision.HIGHEST)
    return features, logits
```

```python
import functools

import jax
import jax.numpy as jnp
import numpy as np
from jax import lax
from jax.experimental import pallas as pl
from jax.experimental.pallas import tpu as pltpu
from jax.sharding import PartitionSpec as P

F32, BF16 = jnp.float32, jnp.bfloat16
LANES = 128
CHUNK = 16
VMEM_LIMIT = 56 * 2**20
PAD = 3


class Plan:
    def __init__(self, channels):
        self.channels = channels
        self.body = channels // LANES * LANES
        self.tail = channels - self.body
        self.bias_at = 3 * self.body + 3 * self.tail
        self.depth = -(-(self.bias_at + 3) // 256) * 256

    def offsets(self, start):
        if start < self.body:
            return start, self.body + start, 2 * self.body + start
        at = 3 * self.body + start - self.body
        return at, at + self.tail, at + 2 * self.tail


def fill_ones(plan, stacked):
    rows = plan.depth - plan.bias_at
    index = lax.broadcasted_iota(jnp.int32, (rows, stacked.shape[1]), 0)
    stacked[plan.bias_at :, :] = jnp.where(index < 3, 1.0, 0.0).astype(BF16)


def depthwise(plan, load, count, taps, stacked, column):
    for start in range(0, plan.channels, CHUNK):
        part = pl.ds(start, CHUNK)
        tap = [taps[part, LANES * j : LANES * (j + 1)] for j in range(9)]
        rows = [jnp.maximum(load(k, part), 0.0) for k in range(count + 2)]
        at = plan.offsets(start)
        for r in range(count):
            left, mid, right = (
                tap[b] * rows[r] + tap[3 + b] * rows[r + 1] + tap[6 + b] * rows[r + 2]
                for b in range(3)
            )
            total = pltpu.roll(left, 1, 1) + mid + pltpu.roll(right, LANES - 1, 1)
            high = total.astype(BF16)
            low = (total - high.astype(F32)).astype(BF16)
            place = pl.ds(column + LANES * r, LANES)
            stacked[pl.ds(at[0], CHUNK), place] = high
            stacked[pl.ds(at[1], CHUNK), place] = high
            stacked[pl.ds(at[2], CHUNK), place] = low


def make_taps(kern, spread, taps):
    taps[...] = jnp.dot(kern[...], spread[...], preferred_element_type=F32)


def triangle_kernel(plan, own, flags, mine, other, mix, kern, spread, carry, rows, taps, stacked, sems):
    step = pl.program_id(0)
    level = step + 1
    odd = flags[0] == 1

    @pl.when(step == 0)
    def _():
        copies = []
        for r in range(own):
            place = jnp.where(odd, r, own - 1 - r)
            copies.append(pltpu.make_async_copy(mine.at[r], rows.at[0, PAD + own + place], sems.at[0]))
            copies.append(pltpu.make_async_copy(other.at[r], rows.at[0, PAD + place], sems.at[0]))
        for copy in copies:
            copy.start()
        fill_ones(plan, stacked)
        make_taps(kern.at[0], spread, taps)
        for copy in copies:
            copy.wait()

    @pl.when(step > 0)
    def _():
        make_taps(kern.at[0], spread, taps)

    source = lax.rem(step, 2)
    target = 1 - source
    top = PAD + 2 * own - 1 - level

    def quad(q, carried):
        first = top - 4 * q - 3
        for p in range(2):
            depthwise(
                plan,
                lambda k, part, p=p: rows[source, first + 2 * p - 1 + k, part, :],
                2, taps, stacked, 256 * p,
            )
        for p in range(2):
            mixed = jnp.dot(mix[0], stacked[:, 256 * p : 256 * (p + 1)], preferred_element_type=F32)
            for r in range(2):
                u = first + 2 * p + r
                rows[target, u] = rows[source, u] + mixed[:, LANES * r : LANES * (r + 1)]
        return carried

    lax.fori_loop(0, (own + 1 - level) // 2, quad, 0)
    carry[0, 0] = rows[target, top - 1]
    carry[0, 1] = rows[target, top]


def triangle(plan, flags, mine, other, mix, kern, spread):
    own, channels, width = mine.shape
    levels = mix.shape[0]
    return pl.pallas_call(
        functools.partial(triangle_kernel, plan, own),
        grid=(levels - 1,),
        out_shape=jax.ShapeDtypeStruct((levels, 2, channels, width), F32),
        in_specs=[
            pl.BlockSpec(memory_space=pltpu.SMEM),
            pl.BlockSpec(memory_space=pl.ANY),
            pl.BlockSpec(memory_space=pl.ANY),
            pl.BlockSpec((1, channels, plan.depth), lambda i: (i, 0, 0)),
            pl.BlockSpec((1, channels, LANES), lambda i: (i, 0, 0)),
            pl.BlockSpec(spread.shape, lambda i: (0, 0)),
        ],
        out_specs=pl.BlockSpec((1, 2, channels, width), lambda i: (i + 1, 0, 0, 0)),
        scratch_shapes=[
            pltpu.VMEM((2, PAD + 2 * own, channels, width), F32),
            pltpu.VMEM((channels, 9 * LANES), F32),
            pltpu.VMEM((plan.depth, 512), BF16),
            pltpu.SemaphoreType.DMA((1,)),
        ],
        compiler_params=pltpu.CompilerParams(vmem_limit_bytes=VMEM_LIMIT),
    )(flags, mine, other, mix, kern, spread)


def wave_kernel(plan, own, start, count, base, order, flags, fresh, behind, mix, kern, spread,
                left_out, last_out, now, taps, stacked):
    step = pl.program_id(0)
    level = start + 1 + step
    odd = flags[0] == 1
    has_next = flags[1] == 1

    @pl.when(step == 0)
    def _():
        fill_ones(plan, stacked)
        for k in range(count):
            if order == "mirror":
                now[k] = fresh[jnp.where(odd, k, count - 1 - k)]
            elif order == "reverse":
                now[k] = fresh[count - 1 - k]
            else:
                now[k] = fresh[k]

    make_taps(kern.at[0], spread, taps)
    left_out[0, 0] = now[count - 2]
    left_out[0, 1] = now[count - 1]

    def load(k, part):
        return behind[0, k, part, :] if k < 2 else now[k - 2, part, :]

    pairs = count // 2
    for p in range(pairs):
        depthwise(plan, lambda k, part, p=p: load(2 * p + k, part), 2, taps, stacked, 256 * p)
    fresh_rows = []
    for p in range(pairs):
        fresh_rows.append(
            jnp.dot(mix[0], stacked[:, 256 * p : 256 * (p + 1)], preferred_element_type=F32)
        )
    for k in reversed(range(count)):
        mixed = fresh_rows[k // 2][:, LANES * (k % 2) : LANES * (k % 2 + 1)]
        old = behind[0, 1] if k == 0 else now[k - 1]
        keep = jnp.logical_or(base - level + k < own, has_next)
        now[k] = jnp.where(keep, old + mixed, 0.0)

    @pl.when(step == pl.num_programs(0) - 1)
    def _():
        for k in range(count):
            last_out[k] = now[k]


def wave(plan, own, start, stop, base, order, flags, fresh, behind, mix, kern, spread):
    count, channels, width = fresh.shape
    whole = lambda i: (0, 0, 0)
    return pl.pallas_call(
        functools.partial(wave_kernel, plan, own, start, count, base, order),
        grid=(stop - start,),
        out_shape=[
            jax.ShapeDtypeStruct(behind.shape, F32),
            jax.ShapeDtypeStruct(fresh.shape, F32),
        ],
        in_specs=[
            pl.BlockSpec(memory_space=pltpu.SMEM),
            pl.BlockSpec(fresh.shape, whole),
            pl.BlockSpec((1, 2, channels, width), lambda i: (start + i, 0, 0, 0)),
            pl.BlockSpec((1, channels, plan.depth), lambda i: (start + i, 0, 0)),
            pl.BlockSpec((1, channels, LANES), lambda i: (start + i, 0, 0)),
            pl.BlockSpec(spread.shape, lambda i: (0, 0)),
        ],
        out_specs=[
            pl.BlockSpec((1, 2, channels, width), lambda i: (start + i, 0, 0, 0)),
            pl.BlockSpec(fresh.shape, whole),
        ],
        scratch_shapes=[
            pltpu.VMEM(fresh.shape, F32),
            pltpu.VMEM((channels, 9 * LANES), F32),
            pltpu.VMEM((plan.depth, LANES * count), BF16),
        ],
        input_output_aliases={2: 0},
        compiler_params=pltpu.CompilerParams(vmem_limit_bytes=VMEM_LIMIT),
    )(flags, fresh, behind, mix, kern, spread)


def split3(values):
    high = lax.reduce_precision(values, 8, 7)
    rest = values - high
    mid = lax.reduce_precision(rest, 8, 7)
    return high, mid, rest - mid


def prepare(plan, kernels, pointwise, biases, odd):
    body = plan.body
    high = lax.reduce_precision(pointwise, 8, 7)
    low = pointwise - high
    shift = jnp.stack(split3(biases), axis=-1)
    mix = jnp.concatenate(
        [
            high[..., :body], low[..., :body], high[..., :body],
            high[..., body:], low[..., body:], high[..., body:], shift,
        ],
        axis=-1,
    )
    mix = jnp.pad(mix, ((0, 0), (0, 0), (0, plan.depth - mix.shape[-1]))).astype(BF16)
    kern = jnp.where(odd, kernels, kernels[:, ::-1])
    kern = kern.reshape(kern.shape[0], 9, plan.channels)
    kern = jnp.concatenate(split3(kern), axis=1)
    kern = jnp.pad(kern, ((0, 0), (0, LANES - 27), (0, 0)))
    kern = jnp.swapaxes(kern, 1, 2).astype(BF16)
    return mix, kern


def spread_matrix():
    spread = np.zeros((LANES, 9, LANES), np.float32)
    for part in range(3):
        for j in range(9):
            spread[9 * part + j, j, :] = 1.0
            if j % 3 == 0:
                spread[9 * part + j, j, LANES - 1] = 0.0
            if j % 3 == 2:
                spread[9 * part + j, j, 0] = 0.0
    return jnp.asarray(spread.reshape(LANES, 9 * LANES), BF16)


def per_device(count, slide_map, kernels, pointwise, biases, classifier):
    own, channels, width = slide_map.shape
    plan = Plan(channels)
    position = lax.axis_index("space")
    odd = position % 2 == 1
    has_next = jnp.logical_and(position > 0, position < count - 1)
    flags = jnp.stack([odd, has_next]).astype(jnp.int32)
    near = [(i, i ^ 1) for i in range(count)]
    far = [(i, i + 1) for i in range(1, count - 1, 2)] + [(i + 1, i) for i in range(1, count - 1, 2)]

    other = lax.ppermute(slide_map, "space", near)
    edge = lax.dynamic_slice_in_dim(slide_map, jnp.where(odd, own - 4, 0), 4, 0)
    halo0 = lax.ppermute(edge, "space", far)
    mix, kern = prepare(plan, kernels, pointwise, biases, odd)
    spread = spread_matrix()

    carry = triangle(plan, flags, slide_map, other, mix, kern, spread)
    halo2 = lax.ppermute(carry[2], "space", far)
    first = jnp.where(odd, slide_map[own - 2 :], slide_map[1::-1])
    carry = lax.dynamic_update_index_in_dim(carry, first, 0, 0)
    carry, mid4 = wave(plan, own, 0, 4, own, "mirror", flags, halo0, carry, mix, kern, spread)
    halo4 = lax.ppermute(mid4[:2], "space", far)
    carry, out0 = wave(plan, own, 4, 8, own, "same", flags, mid4, carry, mix, kern, spread)
    carry, out1 = wave(plan, own, 2, 8, own + 4, "reverse", flags, halo2, carry, mix, kern, spread)
    carry, out2 = wave(plan, own, 4, 8, own + 6, "reverse", flags, halo4, carry, mix, kern, spread)
    features = jnp.concatenate([out0, out1, out2], axis=0)
    features = jnp.where(odd, features, features[::-1])

    sums = jnp.sum(features, axis=(0, 2))
    part = jnp.dot(sums, classifier, precision=lax.Precision.HIGHEST)
    part = part * (1.0 / (own * count * width))
    stride = 1
    while stride < count:
        part = part + lax.ppermute(part, "space", [(i, i ^ stride) for i in range(count)])
        stride *= 2
    return features, part


def solution(mesh):
    in_specs = (P(("groups", "space"), None, None), P(), P(), P(), P())
    out_specs = (P(("groups", "space"), None, None), P("groups"))
    return jax.shard_map(
        functools.partial(per_device, mesh.shape["space"]),
        mesh=mesh, in_specs=in_specs, out_specs=out_specs, check_vma=False,
    )
```

```python
import functools

import jax
import jax.numpy as jnp
import numpy as np
from jax import lax
from jax.experimental import pallas as pl
from jax.experimental.pallas import tpu as pltpu
from jax.sharding import PartitionSpec as P

F32, BF16 = jnp.float32, jnp.bfloat16
LANES = 128
CHUNK = 16
STAGE = 4
VMEM_LIMIT = 56 * 2**20
HBM = pl.BlockSpec(memory_space=pl.ANY)
VMEM = pl.BlockSpec(memory_space=pltpu.VMEM)


class Plan:
    def __init__(self, own, channels, count):
        self.own, self.channels, self.count = own, channels, count
        self.body = channels // LANES * LANES
        self.tail = channels - self.body
        self.tail_at = 3 * self.body
        self.bias_lane = 3 * self.tail
        self.depth = self.tail_at + LANES

    def offsets(self, start):
        if start < self.body:
            return start, self.body + start, 2 * self.body + start
        at = self.tail_at + start - self.body
        return at, at + self.tail, at + 2 * self.tail

    def position(self):
        position = lax.axis_index("space")
        odd = lax.rem(position, 2) == 1
        has_next = jnp.logical_and(position > 0, position < self.count - 1)
        return odd, has_next


def fill_ones(plan, stacked):
    rows = LANES - plan.bias_lane
    index = lax.broadcasted_iota(jnp.int32, (rows, stacked.shape[1]), 0)
    stacked[plan.tail_at + plan.bias_lane :, :] = jnp.where(index < 3, 1.0, 0.0).astype(BF16)


def depthwise(plan, load, taps, stacked, column):
    for start in range(0, plan.channels, CHUNK):
        part = pl.ds(start, CHUNK)
        tap = [taps[part, LANES * j : LANES * (j + 1)] for j in range(9)]
        rows = [jnp.maximum(load(k, part), 0.0) for k in range(4)]
        at = plan.offsets(start)
        for r in range(2):
            left, mid, right = (
                tap[b] * rows[r] + tap[3 + b] * rows[r + 1] + tap[6 + b] * rows[r + 2]
                for b in range(3)
            )
            total = pltpu.roll(left, 1, 1) + mid + pltpu.roll(right, LANES - 1, 1)
            high = total.astype(BF16)
            low = (total - high.astype(F32)).astype(BF16)
            place = pl.ds(column + LANES * r, LANES)
            stacked[pl.ds(at[0], CHUNK), place] = high
            stacked[pl.ds(at[1], CHUNK), place] = high
            stacked[pl.ds(at[2], CHUNK), place] = low


def make_taps(kern, spread, taps):
    high = kern.astype(BF16)
    rest = kern - high.astype(F32)
    mid = rest.astype(BF16)
    low = (rest - mid.astype(F32)).astype(BF16)
    parts = jnp.concatenate([high, mid, low], axis=0)
    taps[...] = lax.dot_general(
        parts, spread, (((0,), (0,)), ((), ())), preferred_element_type=F32
    )


def make_mix(plan, weight, taps, mix):
    body = plan.body
    main = weight[:, :body]
    high = main.astype(BF16)
    mix[:, :body] = high
    mix[:, body : 2 * body] = (main - high.astype(F32)).astype(BF16)
    mix[:, 2 * body : 3 * body] = high
    last = weight[:, body:]
    top = last.astype(BF16).astype(F32)
    rest = jnp.zeros((plan.channels, LANES - 3 * plan.tail), F32)
    tile = jnp.concatenate([top, last - top, top, rest], axis=1)
    mix[:, plan.tail_at :] = (tile + taps[:, 9 * LANES :]).astype(BF16)


def run_level(plan, pairs, load, old, taps, mix, stacked, store, between=None):
    for p in range(pairs):
        depthwise(plan, lambda k, part, p=p: load(2 * p + k, part), taps, stacked, 256 * p)
    if between is not None:
        between()
    for p in range(pairs):
        mixed = jnp.dot(mix[...], stacked[:, 256 * p : 256 * (p + 1)], preferred_element_type=F32)
        for r in range(2):
            k = 2 * p + r
            store(k, old(k) + mixed[:, LANES * r : LANES * (r + 1)])


def edges_kernel(plan, source, near, far, sems):
    odd, _ = plan.position()
    half = source.shape[0] - STAGE
    far_at = jnp.where(odd, half, 0)
    copies = [
        pltpu.make_async_copy(source.at[pl.ds(half - far_at, STAGE)], near, sems.at[0]),
        pltpu.make_async_copy(source.at[pl.ds(far_at, STAGE)], far, sems.at[1]),
    ]
    for copy in copies:
        copy.start()
    for copy in copies:
        copy.wait()


def edges(plan, source):
    shape = jax.ShapeDtypeStruct((STAGE,) + source.shape[1:], F32)
    return pl.pallas_call(
        functools.partial(edges_kernel, plan),
        out_shape=[shape, shape],
        in_specs=[HBM],
        out_specs=[HBM, HBM],
        scratch_shapes=[pltpu.SemaphoreType.DMA((2,))],
    )(source)


def add_rows(sums, rows):
    total = rows[0]
    for row in rows[1:]:
        total = total + row
    sums[...] = total


def trapezoid_kernel(plan, start, *refs):
    first = start == 0
    own, side = plan.own, STAGE
    refs = list(refs)
    inputs = [refs.pop(0) for _ in range(2 if first else 4)]
    weights, kern, spread = refs.pop(0), refs.pop(0), refs.pop(0)
    mixes = refs.pop(0)
    behind = [refs.pop(0) for _ in range(STAGE)]
    final = refs.pop(0)
    sums = None if first else refs.pop(0)
    rows = [refs.pop(0) for _ in range(STAGE + 1)]
    weight, mix, taps, stacked, sem_rows, sem_w, sem_out = refs
    odd, _ = plan.position()

    arrive = []
    for l in range(STAGE):
        copy = pltpu.make_async_copy(weights.at[start + l], weight.at[l], sem_w.at[l])
        if l == 0:
            copy.start()
        arrive.append(copy)
    pieces = []
    if first:
        near, mine = inputs
        for k in range(side):
            pieces.append((near.at[k], jnp.where(odd, k, side - 1 - k)))
        for k in range(own):
            pieces.append((mine.at[k], side + jnp.where(odd, k, own - 1 - k)))
    else:
        near, low, mid, high = inputs
        for k in range(side):
            pieces.append((near.at[k], side - 1 - k))
        at = side
        for piece in (low, mid, high):
            for k in range(piece.shape[0]):
                pieces.append((piece.at[k], at))
                at += 1
    moves = [pltpu.make_async_copy(s, rows[0].at[d], sem_rows.at[i]) for i, (s, d) in enumerate(pieces)]
    for move in moves:
        move.start()
    for copy in arrive[1:]:
        copy.start()
    picked = spread[jnp.where(odd, 1, 0)]
    make_taps(kern[start], picked, taps.at[0])
    for s in range(2):
        fill_ones(plan, stacked.at[s])
    leave = []

    def send(index, source, target):
        copy = pltpu.make_async_copy(source, target, sem_out.at[index])
        copy.start()
        leave.append(copy)

    arrive[0].wait()
    make_mix(plan, weight.at[0], taps.at[0], mix.at[0])
    for move in moves:
        move.wait()
    for l in range(STAGE):
        source, target = rows[l], rows[l + 1]
        count = own + side - 2 * (l + 1)
        send(l, source.at[pl.ds(count, 2)], behind[l])
        send(STAGE + l, mix.at[l], mixes.at[l])

        def store(k, value, target=target):
            target[k] = value

        def between(l=l):
            if l + 1 < STAGE:
                make_taps(kern[start + l + 1], picked, taps.at[(l + 1) % 2])
                arrive[l + 1].wait()
                make_mix(plan, weight.at[l + 1], taps.at[(l + 1) % 2], mix.at[l + 1])

        run_level(
            plan, count // 2,
            lambda k, part, source=source: source[k, part, :],
            lambda k, source=source: source[k + 1],
            taps.at[l % 2], mix.at[l], stacked.at[l % 2], store, between,
        )
    last = rows[STAGE]
    if first:
        send(2 * STAGE, last, final)
    else:
        for k in range(side):
            send(2 * STAGE + k, last.at[k], final.at[jnp.where(odd, k, own - 1 - k)])
        add_rows(sums, [last[k] for k in range(side)])
    for copy in leave:
        copy.wait()


def trapezoid(plan, start, inputs, weights, kern, spread):
    channels, width = plan.channels, inputs[0].shape[-1]
    first = start == 0
    shape = lambda *s: jax.ShapeDtypeStruct(s, F32)
    outs = [jax.ShapeDtypeStruct((STAGE, channels, plan.depth), BF16)]
    outs += [shape(2, channels, width)] * STAGE
    outs += [shape(STAGE if first else plan.own, channels, width)]
    specs = [HBM] * len(outs)
    if not first:
        outs.append(shape(channels, width))
        specs.append(VMEM)
    reach = plan.own + STAGE
    return pl.pallas_call(
        functools.partial(trapezoid_kernel, plan, start),
        out_shape=outs,
        in_specs=[HBM] * (len(inputs) + 1) + [VMEM, VMEM],
        out_specs=specs,
        scratch_shapes=[pltpu.VMEM((reach - 2 * l, channels, width), F32) for l in range(STAGE + 1)]
        + [
            pltpu.VMEM((STAGE, channels, channels), F32),
            pltpu.VMEM((STAGE, channels, plan.depth), BF16),
            pltpu.VMEM((2, channels, 10 * LANES), F32),
            pltpu.VMEM((2, plan.depth, LANES * (reach - 2)), BF16),
            pltpu.SemaphoreType.DMA((reach,)),
            pltpu.SemaphoreType.DMA((STAGE,)),
            pltpu.SemaphoreType.DMA((3 * STAGE,)),
        ],
        compiler_params=pltpu.CompilerParams(vmem_limit_bytes=VMEM_LIMIT),
    )(*inputs, weights, kern, spread)


def wave_kernel(plan, start, stop, count, base, order, keep_from, ending, *refs):
    levels = stop - start
    refs = list(refs)
    fresh = refs.pop(0)
    behind_in = [refs.pop(0) for _ in range(levels)]
    mixes = [refs.pop(0) for _ in range(2)]
    kern, spread = refs.pop(0), refs.pop(0)
    if ending:
        refs.pop(0)
        sums_in = refs.pop(0)
    else:
        sums_in = None
    behind_out = {l: refs.pop(0) for l in range(max(start, keep_from), stop)}
    if ending:
        final, sums = refs.pop(0), refs.pop(0)
    else:
        ends = [refs.pop(0) for _ in range(count // 2)]
    rows = [refs.pop(0) for _ in range(levels + 1)]
    behind, mix, taps, stacked, sem_rows, sem_b, sem_w, sem_out = refs
    odd, has_next = plan.position()

    moves = []
    for k in range(count):
        if order == "mirror":
            place = jnp.where(odd, k, count - 1 - k)
        else:
            place = count - 1 - k
        moves.append(pltpu.make_async_copy(fresh.at[k], rows[0].at[place], sem_rows.at[k]))
    for move in moves:
        move.start()
    tails, weights = [], []
    for l in range(levels):
        tails.append(pltpu.make_async_copy(behind_in[l], behind.at[l], sem_b.at[l]))
        block = start + l
        weights.append(
            pltpu.make_async_copy(mixes[block // STAGE].at[block % STAGE], mix.at[l], sem_w.at[l])
        )
    for l in range(levels):
        tails[l].start()
        weights[l].start()
    picked = spread[jnp.where(odd, 1, 0)]
    make_taps(kern[start], picked, taps.at[0])
    for s in range(2):
        fill_ones(plan, stacked.at[s])
    for move in moves:
        move.wait()
    leave = []

    def send(index, source, target):
        copy = pltpu.make_async_copy(source, target, sem_out.at[index])
        copy.start()
        leave.append(copy)

    for l in range(levels):
        source, target = rows[l], rows[l + 1]
        if start + l in behind_out:
            send(l, source.at[pl.ds(count - 2, 2)], behind_out[start + l])
        tails[l].wait()

        def store(k, value, l=l, target=target):
            if base - (start + l + 1) + k >= plan.own:
                value = jnp.where(has_next, value, 0.0)
            target[k] = value

        def between(l=l):
            if l + 1 < levels:
                make_taps(kern[start + l + 1], picked, taps.at[(l + 1) % 2])
            weights[l].wait()


        run_level(
            plan, count // 2,
            lambda k, part, l=l, source=source: (
                behind[l, k, part, :] if k < 2 else source[k - 2, part, :]
            ),
            lambda k, l=l, source=source: behind[l, 1] if k == 0 else source[k - 1],
            taps.at[l % 2], mix.at[l], stacked.at[l % 2], store, between,
        )
    last = rows[levels]
    if ending:
        for k in range(count):
            u = base - stop + k
            send(levels + k, last.at[k], final.at[jnp.where(odd, u, plan.own - 1 - u)])
        add_rows(sums, [sums_in[...]] + [last[k] for k in range(count)])
    else:
        for p in range(count // 2):
            send(levels + p, last.at[pl.ds(2 * p, 2)], ends[p])
    for copy in leave:
        copy.wait()


def wave(plan, start, stop, base, order, keep_from, fresh, behind, mixes, kern, spread, ending=None):
    count, channels, width = fresh.shape
    levels = stop - start
    pair = jax.ShapeDtypeStruct((2, channels, width), F32)
    outs = [pair] * (stop - max(start, keep_from))
    operands = [fresh, *behind, *mixes, kern, spread]
    in_specs = [HBM] * (len(operands) - 2) + [VMEM, VMEM]
    specs = [HBM] * len(outs)
    aliases = {}
    if ending is not None:
        aliases = {len(operands): len(outs)}
        operands += list(ending)
        in_specs += [HBM, VMEM]
        outs += [jax.ShapeDtypeStruct(e.shape, F32) for e in ending]
        specs += [HBM, VMEM]
    else:
        outs += [pair] * (count // 2)
        specs += [HBM] * (count // 2)
    return pl.pallas_call(
        functools.partial(
            wave_kernel, plan, start, stop, count, base, order, keep_from, ending is not None
        ),
        out_shape=outs,
        in_specs=in_specs,
        out_specs=specs,
        scratch_shapes=[pltpu.VMEM(fresh.shape, F32)] * (levels + 1)
        + [
            pltpu.VMEM((levels, 2, channels, width), F32),
            pltpu.VMEM((levels, channels, plan.depth), BF16),
            pltpu.VMEM((2, channels, 10 * LANES), F32),
            pltpu.VMEM((2, plan.depth, LANES * count), BF16),
            pltpu.SemaphoreType.DMA((count,)),
            pltpu.SemaphoreType.DMA((levels,)),
            pltpu.SemaphoreType.DMA((levels,)),
            pltpu.SemaphoreType.DMA((levels + count,)),
        ],
        input_output_aliases=aliases,
        compiler_params=pltpu.CompilerParams(vmem_limit_bytes=VMEM_LIMIT),
    )(*operands)


def spread_matrix(plan):
    both = np.zeros((2, 3, 16, 10, LANES), np.float32)
    for odd in range(2):
        for part in range(3):
            for a in range(3):
                for b in range(3):
                    row = 3 * (a if odd else 2 - a) + b
                    line = both[odd, part, row, 3 * a + b]
                    line[:] = 1.0
                    if b == 0:
                        line[LANES - 1] = 0.0
                    if b == 2:
                        line[0] = 0.0
            both[odd, part, 9, 9, plan.bias_lane + part] = 1.0
    return jnp.asarray(both.reshape(2, 48, 10 * LANES), BF16)


def per_device(count, slide_map, kernels, pointwise, biases, classifier):
    own, channels, width = slide_map.shape
    levels = kernels.shape[0]
    plan = Plan(own, channels, count)
    near = [(i, i ^ 1) for i in range(count)]
    far = [(i, i + 1) for i in range(1, count - 1, 2)] + [(i + 1, i) for i in range(1, count - 1, 2)]
    send = lambda rows, pairs: lax.ppermute(rows, "space", pairs)

    near0, far0 = edges(plan, slide_map)
    near0, far0 = send(near0, near), send(far0, far)
    kern = jnp.concatenate([kernels.reshape(levels, 9, channels), biases[:, None]], axis=1)
    kern = jnp.pad(kern, ((0, 0), (0, 6), (0, 0)))
    spread = spread_matrix(plan)

    mix0, t0, t1, t2, t3, low4 = trapezoid(plan, 0, [near0, slide_map], pointwise, kern, spread)
    far2 = send(t2, far)
    near4 = send(low4, near)
    w2, w3, mid4, high4 = wave(
        plan, 0, 4, own, "mirror", 2, far0, [t0, t1, t2, t3], [mix0, mix0], kern, spread
    )
    far4 = send(mid4, far)
    mix4, t4, t5, t6, t7, features, sums = trapezoid(
        plan, 4, [near4, low4, mid4, high4], pointwise, kern, spread
    )
    mixes = [mix0, mix4]
    w4, w5, w6, w7, features, sums = wave(
        plan, 2, 8, own + 4, "reverse", 4, far2, [w2, w3, t4, t5, t6, t7], mixes, kern, spread,
        (features, sums),
    )
    features, sums = wave(
        plan, 4, 8, own + 6, "reverse", 8, far4, [w4, w5, w6, w7], mixes, kern, spread,
        (features, sums),
    )
    part = jnp.sum(jnp.sum(sums, axis=1)[:, None] * classifier, axis=0)
    part = part * (1.0 / (own * count * width))
    stride = 1
    while stride < count:
        part = part + send(part, [(i, i ^ stride) for i in range(count)])
        stride *= 2
    return features, part


def solution(mesh):
    in_specs = (P(("groups", "space"), None, None), P(), P(), P(), P())
    out_specs = (P(("groups", "space"), None, None), P("groups"))
    return jax.shard_map(
        functools.partial(per_device, mesh.shape["space"]),
        mesh=mesh, in_specs=in_specs, out_specs=out_specs, check_vma=False,
    )
```

```python
import functools

import jax
import jax.numpy as jnp
from jax import lax
from jax.experimental import pallas as pl
from jax.experimental.pallas import tpu as pltpu
from jax.sharding import PartitionSpec as P

F32, BF16 = jnp.float32, jnp.bfloat16
LANES = 128
CHUNK = 16
STAGE = 4
HBM = pl.BlockSpec(memory_space=pl.ANY)
VMEM = pl.BlockSpec(memory_space=pltpu.VMEM)


class Plan:
    def __init__(self, own, channels, count):
        self.own, self.channels, self.count = own, channels, count
        self.body = channels // LANES * LANES
        self.tail = channels - self.body
        self.tail_at = 3 * self.body
        self.bias_lane = 3 * self.tail
        self.depth = self.tail_at + LANES

    def offsets(self, start):
        if start < self.body:
            return start, self.body + start, 2 * self.body + start
        at = self.tail_at + start - self.body
        return at, at + self.tail, at + 2 * self.tail

    def position(self):
        position = lax.axis_index("space")
        odd = lax.rem(position, 2) == 1
        has_next = jnp.logical_and(position > 0, position < self.count - 1)
        return odd, has_next


def fill_ones(plan, stacked):
    rows = LANES - plan.bias_lane
    index = lax.broadcasted_iota(jnp.int32, (rows, stacked.shape[1]), 0)
    stacked[plan.tail_at + plan.bias_lane :, :] = jnp.where(index < 3, 1.0, 0.0).astype(BF16)


def depthwise(plan, load, taps, stacked, column):
    for start in range(0, plan.channels, CHUNK):
        part = pl.ds(start, CHUNK)
        tap = [taps[part, LANES * j : LANES * (j + 1)] for j in range(9)]
        rows = [jnp.maximum(load(k, part), 0.0) for k in range(4)]
        at = plan.offsets(start)
        for r in range(2):
            left, mid, right = (
                tap[b] * rows[r] + tap[3 + b] * rows[r + 1] + tap[6 + b] * rows[r + 2]
                for b in range(3)
            )
            total = pltpu.roll(left, 1, 1) + mid + pltpu.roll(right, LANES - 1, 1)
            high = total.astype(BF16)
            low = (total - high.astype(F32)).astype(BF16)
            place = pl.ds(column + LANES * r, LANES)
            stacked[pl.ds(at[0], CHUNK), place] = high
            stacked[pl.ds(at[1], CHUNK), place] = high
            stacked[pl.ds(at[2], CHUNK), place] = low


def fill_spread(plan, odd, spread):
    row = lax.broadcasted_iota(jnp.int32, (48, LANES), 0)
    lane = lax.broadcasted_iota(jnp.int32, (48, LANES), 1)
    part, item = row // 16, row % 16
    for a in range(3):
        for b in range(3):
            hit = item == jnp.where(odd, 3 * a + b, 3 * (2 - a) + b)
            if b == 0:
                hit = jnp.logical_and(hit, lane != LANES - 1)
            if b == 2:
                hit = jnp.logical_and(hit, lane != 0)
            at = LANES * (3 * a + b)
            spread[:, at : at + LANES] = jnp.where(hit, 1.0, 0.0).astype(BF16)
    hit = jnp.logical_and(item == 9, lane == plan.bias_lane + part)
    spread[:, 9 * LANES :] = jnp.where(hit, 1.0, 0.0).astype(BF16)


def make_taps(kern, spread, taps):
    high = kern.astype(BF16)
    rest = kern - high.astype(F32)
    mid = rest.astype(BF16)
    low = (rest - mid.astype(F32)).astype(BF16)
    parts = jnp.concatenate([high, mid, low], axis=0)
    taps[...] = lax.dot_general(
        parts, spread, (((0,), (0,)), ((), ())), preferred_element_type=F32
    )


def make_mix(plan, weight, taps, mix):
    body = plan.body
    main = weight[:, :body]
    high = main.astype(BF16)
    mix[:, :body] = high
    mix[:, body : 2 * body] = (main - high.astype(F32)).astype(BF16)
    mix[:, 2 * body : 3 * body] = high
    last = weight[:, body:]
    top = last.astype(BF16).astype(F32)
    rest = jnp.zeros((plan.channels, LANES - 3 * plan.tail), F32)
    tile = jnp.concatenate([top, last - top, top, rest], axis=1)
    mix[:, plan.tail_at :] = (tile + taps[:, 9 * LANES :]).astype(BF16)


def run_level(plan, pairs, load, old, taps, mix, stacked, store, between=None):
    for p in range(pairs):
        depthwise(plan, lambda k, part, p=p: load(2 * p + k, part), taps, stacked, 256 * p)
    if between is not None:
        between()
    for p in range(pairs):
        mixed = jnp.dot(mix[...], stacked[:, 256 * p : 256 * (p + 1)], preferred_element_type=F32)
        for r in range(2):
            k = 2 * p + r
            store(k, old(k) + mixed[:, LANES * r : LANES * (r + 1)])


def edges_kernel(plan, source, near, far, sems):
    odd, _ = plan.position()
    half = source.shape[0] - STAGE
    far_at = jnp.where(odd, half, 0)
    copies = [
        pltpu.make_async_copy(source.at[pl.ds(half - far_at, STAGE)], near, sems.at[0]),
        pltpu.make_async_copy(source.at[pl.ds(far_at, STAGE)], far, sems.at[1]),
    ]
    for copy in copies:
        copy.start()
    for copy in copies:
        copy.wait()


def edges(plan, source):
    shape = jax.ShapeDtypeStruct((STAGE,) + source.shape[1:], F32)
    return pl.pallas_call(
        functools.partial(edges_kernel, plan),
        out_shape=[shape, shape],
        in_specs=[HBM],
        out_specs=[VMEM, VMEM],
        scratch_shapes=[pltpu.SemaphoreType.DMA((2,))],
    )(source)


def add_rows(sums, rows):
    total = rows[0]
    for row in rows[1:]:
        total = total + row
    sums[...] = total


def trapezoid_kernel(plan, start, *refs):
    first = start == 0
    own, side = plan.own, STAGE
    refs = list(refs)
    inputs = [refs.pop(0) for _ in range(2 if first else 4)]
    weights, kern_in = refs.pop(0), refs.pop(0)
    mixes = refs.pop(0)
    behind = [refs.pop(0) for _ in range(STAGE)]
    final = refs.pop(0)
    sums = None if first else refs.pop(0)
    rows = [refs.pop(0) for _ in range(STAGE + 1)]
    kern, spread, weight, mix, taps, stacked, sem_k, sem_rows, sem_w, sem_out = refs
    odd, _ = plan.position()
    taps_in = pltpu.make_async_copy(kern_in.at[pl.ds(start, STAGE)], kern, sem_k.at[0])
    taps_in.start()

    arrive = []
    for l in range(STAGE):
        copy = pltpu.make_async_copy(weights.at[start + l], weight.at[l], sem_w.at[l])
        if l == 0:
            copy.start()
        arrive.append(copy)
    pieces = []
    if first:
        near, mine = inputs
        for k in range(side):
            pieces.append((near.at[k], jnp.where(odd, k, side - 1 - k)))
        for k in range(own):
            pieces.append((mine.at[k], side + jnp.where(odd, k, own - 1 - k)))
    else:
        near, low, mid, high = inputs
        for k in range(side):
            pieces.append((near.at[k], side - 1 - k))
        at = side
        for piece in (low, mid, high):
            for k in range(piece.shape[0]):
                pieces.append((piece.at[k], at))
                at += 1
    moves = [pltpu.make_async_copy(s, rows[0].at[d], sem_rows.at[i]) for i, (s, d) in enumerate(pieces)]
    for move in moves:
        move.start()
    for copy in arrive[1:]:
        copy.start()
    fill_spread(plan, odd, spread)
    for s in range(2):
        fill_ones(plan, stacked.at[s])
    taps_in.wait()
    make_taps(kern[0], spread[...], taps.at[0])
    leave = []

    def send(index, source, target):
        copy = pltpu.make_async_copy(source, target, sem_out.at[index])
        copy.start()
        leave.append(copy)

    arrive[0].wait()
    make_mix(plan, weight.at[0], taps.at[0], mix.at[0])
    for move in moves:
        move.wait()
    for l in range(STAGE):
        source, target = rows[l], rows[l + 1]
        count = own + side - 2 * (l + 1)
        send(l, source.at[pl.ds(count, 2)], behind[l])
        send(STAGE + l, mix.at[l], mixes.at[l])

        def store(k, value, target=target):
            target[k] = value

        def between(l=l):
            if l + 1 < STAGE:
                make_taps(kern[l + 1], spread[...], taps.at[(l + 1) % 2])
                arrive[l + 1].wait()
                make_mix(plan, weight.at[l + 1], taps.at[(l + 1) % 2], mix.at[l + 1])

        run_level(
            plan, count // 2,
            lambda k, part, source=source: source[k, part, :],
            lambda k, source=source: source[k + 1],
            taps.at[l % 2], mix.at[l], stacked.at[l % 2], store, between,
        )
    last = rows[STAGE]
    if first:
        send(2 * STAGE, last, final)
    else:
        for k in range(side):
            send(2 * STAGE + k, last.at[k], final.at[jnp.where(odd, k, own - 1 - k)])
        add_rows(sums, [last[k] for k in range(side)])
    for copy in leave:
        copy.wait()


def trapezoid(plan, start, inputs, weights, kern):
    channels, width = plan.channels, inputs[0].shape[-1]
    first = start == 0
    shape = lambda *s: jax.ShapeDtypeStruct(s, F32)
    outs = [jax.ShapeDtypeStruct((STAGE, channels, plan.depth), BF16)]
    outs += [shape(2, channels, width)] * STAGE
    outs += [shape(STAGE if first else plan.own, channels, width)]
    specs = [HBM] * len(outs)
    if not first:
        outs.append(shape(channels, width))
        specs.append(VMEM)
    reach = plan.own + STAGE
    return pl.pallas_call(
        functools.partial(trapezoid_kernel, plan, start),
        out_shape=outs,
        in_specs=[HBM] * (len(inputs) + 2),
        out_specs=specs,
        scratch_shapes=[pltpu.VMEM((reach - 2 * l, channels, width), F32) for l in range(STAGE + 1)]
        + [
            pltpu.VMEM((STAGE, 16, channels), F32),
            pltpu.VMEM((48, 10 * LANES), BF16),
            pltpu.VMEM((STAGE, channels, channels), F32),
            pltpu.VMEM((STAGE, channels, plan.depth), BF16),
            pltpu.VMEM((2, channels, 10 * LANES), F32),
            pltpu.VMEM((2, plan.depth, LANES * (reach - 2)), BF16),
            pltpu.SemaphoreType.DMA((1,)),
            pltpu.SemaphoreType.DMA((reach,)),
            pltpu.SemaphoreType.DMA((STAGE,)),
            pltpu.SemaphoreType.DMA((3 * STAGE,)),
        ],
        compiler_params=pltpu.CompilerParams(vmem_limit_bytes=36 * 2**20),
    )(*inputs, weights, kern)


def wave_kernel(plan, start, stop, pieces, base, keep_from, ending, *refs):
    levels = stop - start
    refs = list(refs)
    fresh = [refs.pop(0) for _ in pieces]
    behind_in = [refs.pop(0) for _ in range(levels)]
    mixes = [refs.pop(0) for _ in range(2)]
    kern_in = refs.pop(0)
    if ending:
        refs.pop(0)
        sums_in, classes_in = refs.pop(0), refs.pop(0)
    behind_out = {l: refs.pop(0) for l in range(max(start, keep_from), stop)}
    count = sum(rows for rows, _ in pieces)
    if ending:
        final, scores = refs.pop(0), refs.pop(0)
    else:
        ends = [refs.pop(0) for _ in range(count // 2)]
    rows = [refs.pop(0) for _ in range(levels + 1)]
    kern, spread, behind, mix, taps, stacked, sums, classes = refs[:8]
    sem_k, sem_rows, sem_b, sem_w, sem_out = refs[8:]
    odd, has_next = plan.position()

    taps_in = pltpu.make_async_copy(kern_in.at[pl.ds(start, levels)], kern, sem_k.at[0])
    taps_in.start()
    moves = []
    at = 0
    for piece, (size, order) in zip(fresh, pieces):
        for k in range(size):
            if order == "mirror":
                place = jnp.where(odd, k, size - 1 - k)
            elif order == "reverse":
                place = size - 1 - k
            else:
                place = k
            moves.append(
                pltpu.make_async_copy(piece.at[k], rows[0].at[at + place], sem_rows.at[at + k])
            )
        at += size
    for move in moves:
        move.start()
    tails, weights = [], []
    for l in range(levels):
        tails.append(pltpu.make_async_copy(behind_in[l], behind.at[l], sem_b.at[l]))
        block = start + l
        weights.append(
            pltpu.make_async_copy(mixes[block // STAGE].at[block % STAGE], mix.at[l], sem_w.at[l])
        )
    for l in range(min(2, levels)):
        tails[l].start()
        weights[l].start()
    fill_spread(plan, odd, spread)
    for s in range(2):
        fill_ones(plan, stacked.at[s])
    taps_in.wait()
    make_taps(kern[0], spread[...], taps.at[0])
    for move in moves:
        move.wait()
    if ending:
        extra = [
            pltpu.make_async_copy(sums_in, sums, sem_k.at[1]),
            pltpu.make_async_copy(classes_in, classes, sem_k.at[2]),
        ]
        for copy in extra:
            copy.start()
    leave = []

    def send(index, source, target):
        copy = pltpu.make_async_copy(source, target, sem_out.at[index])
        copy.start()
        leave.append(copy)

    for l in range(levels):
        source, target = rows[l], rows[l + 1]
        if start + l in behind_out:
            send(l, source.at[pl.ds(count - 2, 2)], behind_out[start + l])
        tails[l].wait()
        if l + 2 < levels:
            tails[l + 2].start()
            weights[l + 2].start()

        def store(k, value, l=l, target=target):
            if base - (start + l + 1) + k >= plan.own:
                value = jnp.where(has_next, value, 0.0)
            target[k] = value

        def between(l=l):
            if l + 1 < levels:
                make_taps(kern[l + 1], spread[...], taps.at[(l + 1) % 2])
            weights[l].wait()

        run_level(
            plan, count // 2,
            lambda k, part, l=l, source=source: (
                behind[l, k, part, :] if k < 2 else source[k - 2, part, :]
            ),
            lambda k, l=l, source=source: behind[l, 1] if k == 0 else source[k - 1],
            taps.at[l % 2], mix.at[l], stacked.at[l % 2], store, between,
        )
    last = rows[levels]
    if ending:
        for k in range(count):
            u = base - stop + k
            send(levels + k, last.at[k], final.at[jnp.where(odd, u, plan.own - 1 - u)])
        for copy in extra:
            copy.wait()
        add_rows(sums, [sums[...]] + [last[k] for k in range(count)])
        score = jnp.dot(
            classes[...], sums[...], precision=lax.Precision.HIGHEST, preferred_element_type=F32
        )
        scores[...] = jnp.broadcast_to(jnp.sum(score, axis=1, keepdims=True), scores.shape)
    else:
        for p in range(count // 2):
            send(levels + p, last.at[pl.ds(2 * p, 2)], ends[p])
    for copy in leave:
        copy.wait()


def wave(plan, start, stop, base, keep_from, fresh, orders, behind, mixes, kern, ending=None):
    channels, width = fresh[0].shape[1:]
    pieces = tuple((f.shape[0], order) for f, order in zip(fresh, orders))
    count = sum(rows for rows, _ in pieces)
    levels = stop - start
    pair = jax.ShapeDtypeStruct((2, channels, width), F32)
    outs = [pair] * (stop - max(start, keep_from))
    operands = [*fresh, *behind, *mixes, kern]
    specs = [HBM] * len(outs)
    aliases = {}
    if ending is not None:
        aliases = {len(operands): len(outs)}
        operands += list(ending)
        outs += [
            jax.ShapeDtypeStruct(ending[0].shape, F32), jax.ShapeDtypeStruct((8, LANES), F32)
        ]
        specs += [HBM, VMEM]
    else:
        outs += [pair] * (count // 2)
        specs += [HBM] * (count // 2)
    return pl.pallas_call(
        functools.partial(
            wave_kernel, plan, start, stop, pieces, base, keep_from, ending is not None
        ),
        out_shape=outs,
        in_specs=[HBM] * len(operands),
        out_specs=specs,
        scratch_shapes=[pltpu.VMEM((count, channels, width), F32)] * (levels + 1)
        + [
            pltpu.VMEM((levels, 16, channels), F32),
            pltpu.VMEM((48, 10 * LANES), BF16),
            pltpu.VMEM((levels, 2, channels, width), F32),
            pltpu.VMEM((levels, channels, plan.depth), BF16),
            pltpu.VMEM((2, channels, 10 * LANES), F32),
            pltpu.VMEM((2, plan.depth, LANES * count), BF16),
            pltpu.VMEM((channels, width), F32),
            pltpu.VMEM((8, channels), F32),
            pltpu.SemaphoreType.DMA((3,)),
            pltpu.SemaphoreType.DMA((count,)),
            pltpu.SemaphoreType.DMA((levels,)),
            pltpu.SemaphoreType.DMA((levels,)),
            pltpu.SemaphoreType.DMA((levels + count,)),
        ],
        input_output_aliases=aliases,
        compiler_params=pltpu.CompilerParams(vmem_limit_bytes=26 * 2**20),
    )(*operands)


def per_device(count, slide_map, kernels, pointwise, biases, classifier):
    own, channels, width = slide_map.shape
    levels = kernels.shape[0]
    plan = Plan(own, channels, count)
    near = [(i, i ^ 1) for i in range(count)]
    far = [(i, i + 1) for i in range(1, count - 1, 2)] + [(i + 1, i) for i in range(1, count - 1, 2)]
    send = lambda rows, pairs: lax.ppermute(rows, "space", pairs)

    near0, far0 = edges(plan, slide_map)
    near0, far0 = send(near0, near), send(far0, far)
    kern = jnp.concatenate([kernels.reshape(levels, 9, channels), biases[:, None]], axis=1)
    kern = jnp.pad(kern, ((0, 0), (0, 6), (0, 0)))

    mix0, t0, t1, t2, t3, low4 = trapezoid(plan, 0, [near0, slide_map], pointwise, kern)
    far2 = send(t2, far)
    near4 = send(low4, near)
    w2, w3, mid4, high4 = wave(
        plan, 0, 4, own, 2, [far0], ["mirror"], [t0, t1, t2, t3], [mix0, mix0], kern
    )
    far4 = send(mid4, far)
    mix4, t4, t5, t6, t7, features, sums = trapezoid(
        plan, 4, [near4, low4, mid4, high4], pointwise, kern
    )
    mixes = [mix0, mix4]
    (next4,) = wave(plan, 2, 4, own + 4, 4, [far2], ["reverse"], [w2, w3], mixes, kern)
    classes = jnp.pad(classifier.T, ((0, 8 - classifier.shape[1]), (0, 0)))
    features, part = wave(
        plan, 4, 8, own + 4, 8, [next4, far4], ["same", "reverse"], [t4, t5, t6, t7], mixes, kern,
        (features, sums, classes),
    )
    stride = 1
    while stride < count:
        part = part + send(part, [(i, i ^ stride) for i in range(count)])
        stride *= 2
    return features, part[: classifier.shape[1], 0] * (1.0 / (own * count * width))


def solution(mesh):
    in_specs = (P(("groups", "space"), None, None), P(), P(), P(), P())
    out_specs = (P(("groups", "space"), None, None), P("groups"))
    return jax.shard_map(
        functools.partial(per_device, mesh.shape["space"]),
        mesh=mesh, in_specs=in_specs, out_specs=out_specs, check_vma=False,
    )
```

```python
import functools

import jax
import jax.numpy as jnp
from jax import lax
from jax.experimental import pallas as pl
from jax.experimental.pallas import tpu as pltpu
from jax.sharding import PartitionSpec as P

F32, BF16 = jnp.float32, jnp.bfloat16
LANES = 128
CHUNK = 16
STAGE = 4
HBM = pl.BlockSpec(memory_space=pl.ANY)
VMEM = pl.BlockSpec(memory_space=pltpu.VMEM)


class Plan:
    def __init__(self, own, channels, count):
        self.own, self.channels, self.count = own, channels, count
        self.body = channels // LANES * LANES
        self.tail = channels - self.body
        self.tail_at = 3 * self.body
        self.bias_lane = 3 * self.tail
        self.depth = self.tail_at + LANES

    def offsets(self, start):
        if start < self.body:
            return start, self.body + start, 2 * self.body + start
        at = self.tail_at + start - self.body
        return at, at + self.tail, at + 2 * self.tail

    def position(self):
        position = lax.axis_index("space")
        odd = lax.rem(position, 2) == 1
        has_next = jnp.logical_and(position > 0, position < self.count - 1)
        return odd, has_next


def fill_ones(plan, stacked):
    rows = LANES - plan.bias_lane
    index = lax.broadcasted_iota(jnp.int32, (rows, stacked.shape[1]), 0)
    stacked[plan.tail_at + plan.bias_lane :, :] = jnp.where(index < 3, 1.0, 0.0).astype(BF16)


def depthwise(plan, load, taps, stacked, column):
    for start in range(0, plan.channels, CHUNK):
        part = pl.ds(start, CHUNK)
        tap = [taps[part, LANES * j : LANES * (j + 1)] for j in range(9)]
        rows = [jnp.maximum(load(k, part), 0.0) for k in range(4)]
        at = plan.offsets(start)
        for r in range(2):
            left, mid, right = (
                tap[b] * rows[r] + tap[3 + b] * rows[r + 1] + tap[6 + b] * rows[r + 2]
                for b in range(3)
            )
            total = pltpu.roll(left, 1, 1) + mid + pltpu.roll(right, LANES - 1, 1)
            high = total.astype(BF16)
            low = (total - high.astype(F32)).astype(BF16)
            place = pl.ds(column + LANES * r, LANES)
            stacked[pl.ds(at[0], CHUNK), place] = high
            stacked[pl.ds(at[1], CHUNK), place] = high
            stacked[pl.ds(at[2], CHUNK), place] = low


def fill_spread(plan, odd, spread):
    row = lax.broadcasted_iota(jnp.int32, (48, LANES), 0)
    lane = lax.broadcasted_iota(jnp.int32, (48, LANES), 1)
    part, item = row // 16, row % 16
    for a in range(3):
        for b in range(3):
            hit = item == jnp.where(odd, 3 * a + b, 3 * (2 - a) + b)
            if b == 0:
                hit = jnp.logical_and(hit, lane != LANES - 1)
            if b == 2:
                hit = jnp.logical_and(hit, lane != 0)
            at = LANES * (3 * a + b)
            spread[:, at : at + LANES] = jnp.where(hit, 1.0, 0.0).astype(BF16)
    hit = jnp.logical_and(item == 9, lane == plan.bias_lane + part)
    spread[:, 9 * LANES :] = jnp.where(hit, 1.0, 0.0).astype(BF16)


def make_taps(kern, spread, taps):
    high = kern.astype(BF16)
    rest = kern - high.astype(F32)
    mid = rest.astype(BF16)
    low = (rest - mid.astype(F32)).astype(BF16)
    parts = jnp.concatenate([high, mid, low], axis=0)
    taps[...] = lax.dot_general(
        parts, spread, (((0,), (0,)), ((), ())), preferred_element_type=F32
    )


def make_mix(plan, weight, taps, mix):
    body = plan.body
    main = weight[:, :body]
    high = main.astype(BF16)
    mix[:, :body] = high
    mix[:, body : 2 * body] = (main - high.astype(F32)).astype(BF16)
    mix[:, 2 * body : 3 * body] = high
    last = weight[:, body:]
    top = last.astype(BF16).astype(F32)
    rest = jnp.zeros((plan.channels, LANES - 3 * plan.tail), F32)
    tile = jnp.concatenate([top, last - top, top, rest], axis=1)
    mix[:, plan.tail_at :] = (tile + taps[:, 9 * LANES :]).astype(BF16)


def run_level(plan, pairs, load, old, taps, mix, stacked, store, between=None):
    def product(p):
        mixed = jnp.dot(mix[...], stacked[:, 256 * p : 256 * (p + 1)], preferred_element_type=F32)
        for r in range(2):
            k = 2 * p + r
            store(k, old(k) + mixed[:, LANES * r : LANES * (r + 1)])

    for p in range(pairs):
        depthwise(plan, lambda k, part, p=p: load(2 * p + k, part), taps, stacked, 256 * p)
        if p == 0 and between is not None:
            between()
        if p > 0:
            product(p - 1)
    product(pairs - 1)


def edges_kernel(plan, source, near, far, sems):
    odd, _ = plan.position()
    half = source.shape[0] - STAGE
    far_at = jnp.where(odd, half, 0)
    copies = [
        pltpu.make_async_copy(source.at[pl.ds(half - far_at, STAGE)], near, sems.at[0]),
        pltpu.make_async_copy(source.at[pl.ds(far_at, STAGE)], far, sems.at[1]),
    ]
    for copy in copies:
        copy.start()
    for copy in copies:
        copy.wait()


def edges(plan, source):
    shape = jax.ShapeDtypeStruct((STAGE,) + source.shape[1:], F32)
    return pl.pallas_call(
        functools.partial(edges_kernel, plan),
        out_shape=[shape, shape],
        in_specs=[HBM],
        out_specs=[VMEM, VMEM],
        scratch_shapes=[pltpu.SemaphoreType.DMA((2,))],
    )(source)


def add_rows(sums, rows):
    total = rows[0]
    for row in rows[1:]:
        total = total + row
    sums[...] = total


def trapezoid_kernel(plan, start, *refs):
    first = start == 0
    own, side = plan.own, STAGE
    refs = list(refs)
    inputs = [refs.pop(0) for _ in range(2 if first else 4)]
    weights, kern_in = refs.pop(0), refs.pop(0)
    mixes = refs.pop(0)
    behind = [refs.pop(0) for _ in range(STAGE)]
    final = refs.pop(0)
    sums = None if first else refs.pop(0)
    rows = [refs.pop(0) for _ in range(STAGE + 1)]
    kern, spread, weight, mix, taps, stacked, sem_k, sem_rows, sem_w, sem_out = refs
    odd, _ = plan.position()
    taps_in = pltpu.make_async_copy(kern_in.at[pl.ds(start, STAGE)], kern, sem_k.at[0])
    taps_in.start()

    arrive = []
    for l in range(STAGE):
        copy = pltpu.make_async_copy(weights.at[start + l], weight.at[l], sem_w.at[l])
        if l == 0:
            copy.start()
        arrive.append(copy)
    pieces = []
    if first:
        near, mine = inputs
        for k in range(side):
            pieces.append((near.at[k], jnp.where(odd, k, side - 1 - k)))
        for k in range(own):
            pieces.append((mine.at[k], side + jnp.where(odd, k, own - 1 - k)))
    else:
        near, low, mid, high = inputs
        for k in range(side):
            pieces.append((near.at[k], side - 1 - k))
        at = side
        for piece in (low, mid, high):
            for k in range(piece.shape[0]):
                pieces.append((piece.at[k], at))
                at += 1
    moves = [pltpu.make_async_copy(s, rows[0].at[d], sem_rows.at[i]) for i, (s, d) in enumerate(pieces)]
    for move in moves:
        move.start()
    for copy in arrive[1:]:
        copy.start()
    fill_spread(plan, odd, spread)
    for s in range(2):
        fill_ones(plan, stacked.at[s])
    taps_in.wait()
    make_taps(kern[0], spread[...], taps.at[0])
    leave = []

    def send(index, source, target):
        copy = pltpu.make_async_copy(source, target, sem_out.at[index])
        copy.start()
        leave.append(copy)

    arrive[0].wait()
    make_mix(plan, weight.at[0], taps.at[0], mix.at[0])
    for move in moves:
        move.wait()
    for l in range(STAGE):
        source, target = rows[l], rows[l + 1]
        count = own + side - 2 * (l + 1)
        send(l, source.at[pl.ds(count, 2)], behind[l])
        send(STAGE + l, mix.at[l], mixes.at[l])

        def store(k, value, target=target):
            target[k] = value

        def between(l=l):
            if l + 1 < STAGE:
                make_taps(kern[l + 1], spread[...], taps.at[(l + 1) % 2])
                arrive[l + 1].wait()
                make_mix(plan, weight.at[l + 1], taps.at[(l + 1) % 2], mix.at[l + 1])

        run_level(
            plan, count // 2,
            lambda k, part, source=source: source[k, part, :],
            lambda k, source=source: source[k + 1],
            taps.at[l % 2], mix.at[l], stacked.at[l % 2], store, between,
        )
    last = rows[STAGE]
    if first:
        send(2 * STAGE, last, final)
    else:
        for k in range(side):
            send(2 * STAGE + k, last.at[k], final.at[jnp.where(odd, k, own - 1 - k)])
        add_rows(sums, [last[k] for k in range(side)])
    for copy in leave:
        copy.wait()


def trapezoid(plan, start, inputs, weights, kern):
    channels, width = plan.channels, inputs[0].shape[-1]
    first = start == 0
    shape = lambda *s: jax.ShapeDtypeStruct(s, F32)
    outs = [jax.ShapeDtypeStruct((STAGE, channels, plan.depth), BF16)]
    outs += [shape(2, channels, width)] * STAGE
    outs += [shape(STAGE if first else plan.own, channels, width)]
    specs = [HBM] * len(outs)
    if not first:
        outs.append(shape(channels, width))
        specs.append(VMEM)
    reach = plan.own + STAGE
    return pl.pallas_call(
        functools.partial(trapezoid_kernel, plan, start),
        out_shape=outs,
        in_specs=[HBM] * (len(inputs) + 2),
        out_specs=specs,
        scratch_shapes=[pltpu.VMEM((reach - 2 * l, channels, width), F32) for l in range(STAGE + 1)]
        + [
            pltpu.VMEM((STAGE, 16, channels), F32),
            pltpu.VMEM((48, 10 * LANES), BF16),
            pltpu.VMEM((STAGE, channels, channels), F32),
            pltpu.VMEM((STAGE, channels, plan.depth), BF16),
            pltpu.VMEM((2, channels, 10 * LANES), F32),
            pltpu.VMEM((2, plan.depth, LANES * (reach - 2)), BF16),
            pltpu.SemaphoreType.DMA((1,)),
            pltpu.SemaphoreType.DMA((reach,)),
            pltpu.SemaphoreType.DMA((STAGE,)),
            pltpu.SemaphoreType.DMA((3 * STAGE,)),
        ],
        compiler_params=pltpu.CompilerParams(vmem_limit_bytes=56 * 2**20),
    )(*inputs, weights, kern)


def wave_kernel(plan, start, stop, pieces, base, keep_from, ending, *refs):
    levels = stop - start
    refs = list(refs)
    fresh = [refs.pop(0) for _ in pieces]
    behind_in = [refs.pop(0) for _ in range(levels)]
    mixes = [refs.pop(0) for _ in range(2)]
    kern_in = refs.pop(0)
    if ending:
        refs.pop(0)
        sums_in, classes_in = refs.pop(0), refs.pop(0)
    behind_out = {l: refs.pop(0) for l in range(max(start, keep_from), stop)}
    count = sum(rows for rows, _ in pieces)
    if ending:
        final, scores = refs.pop(0), refs.pop(0)
    else:
        ends = [refs.pop(0) for _ in range(count // 2)]
    rows = [refs.pop(0) for _ in range(levels + 1)]
    kern, spread, behind, mix, taps, stacked, sums, classes = refs[:8]
    sem_k, sem_rows, sem_b, sem_w, sem_out = refs[8:]
    odd, has_next = plan.position()

    taps_in = pltpu.make_async_copy(kern_in.at[pl.ds(start, levels)], kern, sem_k.at[0])
    taps_in.start()
    moves = []
    at = 0
    for piece, (size, order) in zip(fresh, pieces):
        for k in range(size):
            if order == "mirror":
                place = jnp.where(odd, k, size - 1 - k)
            elif order == "reverse":
                place = size - 1 - k
            else:
                place = k
            moves.append(
                pltpu.make_async_copy(piece.at[k], rows[0].at[at + place], sem_rows.at[at + k])
            )
        at += size
    for move in moves:
        move.start()
    tails, weights = [], []
    for l in range(levels):
        tails.append(pltpu.make_async_copy(behind_in[l], behind.at[l], sem_b.at[l]))
        block = start + l
        weights.append(
            pltpu.make_async_copy(mixes[block // STAGE].at[block % STAGE], mix.at[l], sem_w.at[l])
        )
    for l in range(min(2, levels)):
        tails[l].start()
        weights[l].start()
    fill_spread(plan, odd, spread)
    for s in range(2):
        fill_ones(plan, stacked.at[s])
    taps_in.wait()
    make_taps(kern[0], spread[...], taps.at[0])
    for move in moves:
        move.wait()
    if ending:
        extra = [
            pltpu.make_async_copy(sums_in, sums, sem_k.at[1]),
            pltpu.make_async_copy(classes_in, classes, sem_k.at[2]),
        ]
        for copy in extra:
            copy.start()
    leave = []

    def send(index, source, target):
        copy = pltpu.make_async_copy(source, target, sem_out.at[index])
        copy.start()
        leave.append(copy)

    for l in range(levels):
        source, target = rows[l], rows[l + 1]
        if start + l in behind_out:
            send(l, source.at[pl.ds(count - 2, 2)], behind_out[start + l])
        tails[l].wait()
        if l + 2 < levels:
            tails[l + 2].start()
            weights[l + 2].start()

        def store(k, value, l=l, target=target):
            if base - (start + l + 1) + k >= plan.own:
                value = jnp.where(has_next, value, 0.0)
            target[k] = value

        def between(l=l):
            if l + 1 < levels:
                make_taps(kern[l + 1], spread[...], taps.at[(l + 1) % 2])
            weights[l].wait()

        run_level(
            plan, count // 2,
            lambda k, part, l=l, source=source: (
                behind[l, k, part, :] if k < 2 else source[k - 2, part, :]
            ),
            lambda k, l=l, source=source: behind[l, 1] if k == 0 else source[k - 1],
            taps.at[l % 2], mix.at[l], stacked.at[l % 2], store, between,
        )
    last = rows[levels]
    if ending:
        for k in range(count):
            u = base - stop + k
            send(levels + k, last.at[k], final.at[jnp.where(odd, u, plan.own - 1 - u)])
        for copy in extra:
            copy.wait()
        add_rows(sums, [sums[...]] + [last[k] for k in range(count)])
        score = jnp.dot(
            classes[...], sums[...], precision=lax.Precision.HIGHEST, preferred_element_type=F32
        )
        scores[...] = jnp.broadcast_to(jnp.sum(score, axis=1, keepdims=True), scores.shape)
    else:
        for p in range(count // 2):
            send(levels + p, last.at[pl.ds(2 * p, 2)], ends[p])
    for copy in leave:
        copy.wait()


def wave(plan, start, stop, base, keep_from, fresh, orders, behind, mixes, kern, ending=None):
    channels, width = fresh[0].shape[1:]
    pieces = tuple((f.shape[0], order) for f, order in zip(fresh, orders))
    count = sum(rows for rows, _ in pieces)
    levels = stop - start
    pair = jax.ShapeDtypeStruct((2, channels, width), F32)
    outs = [pair] * (stop - max(start, keep_from))
    operands = [*fresh, *behind, *mixes, kern]
    specs = [HBM] * len(outs)
    aliases = {}
    if ending is not None:
        aliases = {len(operands): len(outs)}
        operands += list(ending)
        outs += [
            jax.ShapeDtypeStruct(ending[0].shape, F32), jax.ShapeDtypeStruct((8, LANES), F32)
        ]
        specs += [HBM, VMEM]
    else:
        outs += [pair] * (count // 2)
        specs += [HBM] * (count // 2)
    return pl.pallas_call(
        functools.partial(
            wave_kernel, plan, start, stop, pieces, base, keep_from, ending is not None
        ),
        out_shape=outs,
        in_specs=[HBM] * len(operands),
        out_specs=specs,
        scratch_shapes=[pltpu.VMEM((count, channels, width), F32)] * (levels + 1)
        + [
            pltpu.VMEM((levels, 16, channels), F32),
            pltpu.VMEM((48, 10 * LANES), BF16),
            pltpu.VMEM((levels, 2, channels, width), F32),
            pltpu.VMEM((levels, channels, plan.depth), BF16),
            pltpu.VMEM((2, channels, 10 * LANES), F32),
            pltpu.VMEM((2, plan.depth, LANES * count), BF16),
            pltpu.VMEM((channels, width), F32),
            pltpu.VMEM((8, channels), F32),
            pltpu.SemaphoreType.DMA((3,)),
            pltpu.SemaphoreType.DMA((count,)),
            pltpu.SemaphoreType.DMA((levels,)),
            pltpu.SemaphoreType.DMA((levels,)),
            pltpu.SemaphoreType.DMA((levels + count,)),
        ],
        input_output_aliases=aliases,
        compiler_params=pltpu.CompilerParams(vmem_limit_bytes=56 * 2**20),
    )(*operands)


def per_device(count, slide_map, kernels, pointwise, biases, classifier):
    own, channels, width = slide_map.shape
    levels = kernels.shape[0]
    plan = Plan(own, channels, count)
    near = [(i, i ^ 1) for i in range(count)]
    far = [(i, i + 1) for i in range(1, count - 1, 2)] + [(i + 1, i) for i in range(1, count - 1, 2)]
    send = lambda rows, pairs: lax.ppermute(rows, "space", pairs)

    near0, far0 = edges(plan, slide_map)
    near0, far0 = send(near0, near), send(far0, far)
    kern = jnp.concatenate([kernels.reshape(levels, 9, channels), biases[:, None]], axis=1)
    kern = jnp.pad(kern, ((0, 0), (0, 6), (0, 0)))

    mix0, t0, t1, t2, t3, low4 = trapezoid(plan, 0, [near0, slide_map], pointwise, kern)
    far2 = send(t2, far)
    near4 = send(low4, near)
    w2, w3, mid4, high4 = wave(
        plan, 0, 4, own, 2, [far0], ["mirror"], [t0, t1, t2, t3], [mix0, mix0], kern
    )
    far4 = send(mid4, far)
    mix4, t4, t5, t6, t7, features, sums = trapezoid(
        plan, 4, [near4, low4, mid4, high4], pointwise, kern
    )
    mixes = [mix0, mix4]
    (next4,) = wave(plan, 2, 4, own + 4, 4, [far2], ["reverse"], [w2, w3], mixes, kern)
    classes = jnp.pad(classifier.T, ((0, 8 - classifier.shape[1]), (0, 0)))
    features, part = wave(
        plan, 4, 8, own + 4, 8, [next4, far4], ["same", "reverse"], [t4, t5, t6, t7], mixes, kern,
        (features, sums, classes),
    )
    stride = 1
    while stride < count:
        part = part + send(part, [(i, i ^ stride) for i in range(count)])
        stride *= 2
    return features, part[: classifier.shape[1], 0] * (1.0 / (own * count * width))


def solution(mesh):
    in_specs = (P(("groups", "space"), None, None), P(), P(), P(), P())
    out_specs = (P(("groups", "space"), None, None), P("groups"))
    return jax.shard_map(
        functools.partial(per_device, mesh.shape["space"]),
        mesh=mesh, in_specs=in_specs, out_specs=out_specs, check_vma=False,
    )
```

```python
import functools

import jax
import jax.numpy as jnp
from jax import lax
from jax.experimental import pallas as pl
from jax.experimental.pallas import tpu as pltpu
from jax.sharding import PartitionSpec as P

F32, BF16 = jnp.float32, jnp.bfloat16
LANES = 128
CHUNK = 16
STAGE = 4
HBM = pl.BlockSpec(memory_space=pl.ANY)
VMEM = pl.BlockSpec(memory_space=pltpu.VMEM)


class Plan:
    def __init__(self, own, channels, count):
        self.own, self.channels, self.count = own, channels, count
        self.body = channels // LANES * LANES
        self.tail = channels - self.body
        self.tail_at = 3 * self.body
        self.bias_lane = 3 * self.tail
        self.depth = self.tail_at + LANES

    def offsets(self, start):
        if start < self.body:
            return start, self.body + start, 2 * self.body + start
        at = self.tail_at + start - self.body
        return at, at + self.tail, at + 2 * self.tail

    def position(self):
        position = lax.axis_index("space")
        odd = lax.rem(position, 2) == 1
        has_next = jnp.logical_and(position > 0, position < self.count - 1)
        return odd, has_next


def fill_ones(plan, stacked):
    rows = LANES - plan.bias_lane
    index = lax.broadcasted_iota(jnp.int32, (rows, stacked.shape[1]), 0)
    stacked[plan.tail_at + plan.bias_lane :, :] = jnp.where(index < 3, 1.0, 0.0).astype(BF16)


def depthwise(plan, load, taps, stacked, column):
    for start in range(0, plan.channels, CHUNK):
        part = pl.ds(start, CHUNK)
        tap = [taps[part, LANES * j : LANES * (j + 1)] for j in range(9)]
        rows = [jnp.maximum(load(k, part), 0.0) for k in range(4)]
        at = plan.offsets(start)
        for r in range(2):
            left, mid, right = (
                tap[b] * rows[r] + tap[3 + b] * rows[r + 1] + tap[6 + b] * rows[r + 2]
                for b in range(3)
            )
            total = pltpu.roll(left, 1, 1) + mid + pltpu.roll(right, LANES - 1, 1)
            high = total.astype(BF16)
            low = (total - high.astype(F32)).astype(BF16)
            place = pl.ds(column + LANES * r, LANES)
            stacked[pl.ds(at[0], CHUNK), place] = high
            stacked[pl.ds(at[1], CHUNK), place] = high
            stacked[pl.ds(at[2], CHUNK), place] = low


def fill_spread(plan, odd, spread):
    row = lax.broadcasted_iota(jnp.int32, (48, LANES), 0)
    lane = lax.broadcasted_iota(jnp.int32, (48, LANES), 1)
    part, item = row // 16, row % 16
    for a in range(3):
        for b in range(3):
            hit = item == jnp.where(odd, 3 * a + b, 3 * (2 - a) + b)
            if b == 0:
                hit = jnp.logical_and(hit, lane != LANES - 1)
            if b == 2:
                hit = jnp.logical_and(hit, lane != 0)
            at = LANES * (3 * a + b)
            spread[:, at : at + LANES] = jnp.where(hit, 1.0, 0.0).astype(BF16)
    hit = jnp.logical_and(item == 9, lane == plan.bias_lane + part)
    spread[:, 9 * LANES :] = jnp.where(hit, 1.0, 0.0).astype(BF16)


def make_taps(kern, spread, taps):
    high = kern.astype(BF16)
    rest = kern - high.astype(F32)
    mid = rest.astype(BF16)
    low = (rest - mid.astype(F32)).astype(BF16)
    parts = jnp.concatenate([high, mid, low], axis=0)
    taps[...] = lax.dot_general(
        parts, spread, (((0,), (0,)), ((), ())), preferred_element_type=F32
    )


def make_mix(plan, weight, taps, mix):
    body = plan.body
    main = weight[:, :body]
    high = main.astype(BF16)
    mix[:, :body] = high
    mix[:, body : 2 * body] = (main - high.astype(F32)).astype(BF16)
    mix[:, 2 * body : 3 * body] = high
    last = weight[:, body:]
    top = last.astype(BF16).astype(F32)
    rest = jnp.zeros((plan.channels, LANES - 3 * plan.tail), F32)
    tile = jnp.concatenate([top, last - top, top, rest], axis=1)
    mix[:, plan.tail_at :] = (tile + taps[:, 9 * LANES :]).astype(BF16)


def run_level(plan, pairs, load, old, taps, mix, stacked, store, between=None):
    def product(p):
        mixed = jnp.dot(mix[...], stacked[:, 256 * p : 256 * (p + 1)], preferred_element_type=F32)
        for r in range(2):
            k = 2 * p + r
            store(k, old(k) + mixed[:, LANES * r : LANES * (r + 1)])

    for p in range(pairs):
        depthwise(plan, lambda k, part, p=p: load(2 * p + k, part), taps, stacked, 256 * p)
        if p == 0 and between is not None:
            between()
        if p > 0:
            product(p - 1)
    product(pairs - 1)


def edges_kernel(plan, source, near, far, sems):
    odd, _ = plan.position()
    half = source.shape[0] - STAGE
    far_at = jnp.where(odd, half, 0)
    copies = [
        pltpu.make_async_copy(source.at[pl.ds(half - far_at, STAGE)], near, sems.at[0]),
        pltpu.make_async_copy(source.at[pl.ds(far_at, STAGE)], far, sems.at[1]),
    ]
    for copy in copies:
        copy.start()
    for copy in copies:
        copy.wait()


def edges(plan, source):
    shape = jax.ShapeDtypeStruct((STAGE,) + source.shape[1:], F32)
    return pl.pallas_call(
        functools.partial(edges_kernel, plan),
        out_shape=[shape, shape],
        in_specs=[HBM],
        out_specs=[VMEM, VMEM],
        scratch_shapes=[pltpu.SemaphoreType.DMA((2,))],
    )(source)


def add_rows(sums, rows):
    total = rows[0]
    for row in rows[1:]:
        total = total + row
    sums[...] = total


def trapezoid_kernel(plan, start, *refs):
    first = start == 0
    own, side = plan.own, STAGE
    refs = list(refs)
    inputs = [refs.pop(0) for _ in range(2 if first else 4)]
    weights, kern_in = refs.pop(0), refs.pop(0)
    mixes = refs.pop(0)
    behind = [refs.pop(0) for _ in range(STAGE)]
    final = refs.pop(0)
    sums = None if first else refs.pop(0)
    rows = [refs.pop(0) for _ in range(STAGE + 1)]
    kern, spread, weight, mix, taps, stacked, sem_k, sem_rows, sem_w, sem_out = refs
    odd, _ = plan.position()
    taps_in = pltpu.make_async_copy(kern_in.at[pl.ds(start, STAGE)], kern, sem_k.at[0])
    taps_in.start()

    arrive = []
    for l in range(STAGE):
        copy = pltpu.make_async_copy(weights.at[start + l], weight.at[l], sem_w.at[l])
        if l == 0:
            copy.start()
        arrive.append(copy)
    pieces = []
    if first:
        near, mine = inputs
        for k in range(side):
            pieces.append((near.at[k], jnp.where(odd, k, side - 1 - k)))
        for k in range(own):
            pieces.append((mine.at[k], side + jnp.where(odd, k, own - 1 - k)))
    else:
        near, low, mid, high = inputs
        for k in range(side):
            pieces.append((near.at[k], side - 1 - k))
        at = side
        for piece in (low, mid, high):
            for k in range(piece.shape[0]):
                pieces.append((piece.at[k], at))
                at += 1
    moves = [pltpu.make_async_copy(s, rows[0].at[d], sem_rows.at[i]) for i, (s, d) in enumerate(pieces)]
    for move in moves:
        move.start()
    for copy in arrive[1:]:
        copy.start()
    fill_spread(plan, odd, spread)
    for s in range(2):
        fill_ones(plan, stacked.at[s])
    taps_in.wait()
    make_taps(kern[0], spread[...], taps.at[0])
    leave = []

    def send(index, source, target):
        copy = pltpu.make_async_copy(source, target, sem_out.at[index])
        copy.start()
        leave.append(copy)

    arrive[0].wait()
    make_mix(plan, weight.at[0], taps.at[0], mix.at[0])
    for move in moves:
        move.wait()
    for l in range(STAGE):
        source, target = rows[l], rows[l + 1]
        count = own + side - 2 * (l + 1)
        send(l, source.at[pl.ds(count, 2)], behind[l])
        send(STAGE + l, mix.at[l], mixes.at[l])

        def store(k, value, target=target):
            target[k] = value

        def between(l=l):
            if l + 1 < STAGE:
                make_taps(kern[l + 1], spread[...], taps.at[(l + 1) % 2])
                arrive[l + 1].wait()
                make_mix(plan, weight.at[l + 1], taps.at[(l + 1) % 2], mix.at[l + 1])

        run_level(
            plan, count // 2,
            lambda k, part, source=source: source[k, part, :],
            lambda k, source=source: source[k + 1],
            taps.at[l % 2], mix.at[l], stacked.at[l % 2], store, between,
        )
    last = rows[STAGE]
    if first:
        send(2 * STAGE, last, final)
    else:
        for k in range(side):
            send(2 * STAGE + k, last.at[k], final.at[jnp.where(odd, k, own - 1 - k)])
        add_rows(sums, [last[k] for k in range(side)])
    for copy in leave:
        copy.wait()


def trapezoid(plan, start, inputs, weights, kern):
    channels, width = plan.channels, inputs[0].shape[-1]
    first = start == 0
    shape = lambda *s: jax.ShapeDtypeStruct(s, F32)
    outs = [jax.ShapeDtypeStruct((STAGE, channels, plan.depth), BF16)]
    outs += [shape(2, channels, width)] * STAGE
    outs += [shape(STAGE if first else plan.own, channels, width)]
    specs = [HBM] * len(outs)
    if not first:
        outs.append(shape(channels, width))
        specs.append(VMEM)
    reach = plan.own + STAGE
    return pl.pallas_call(
        functools.partial(trapezoid_kernel, plan, start),
        out_shape=outs,
        in_specs=[HBM] * (len(inputs) + 2),
        out_specs=specs,
        scratch_shapes=[pltpu.VMEM((reach - 2 * l, channels, width), F32) for l in range(STAGE + 1)]
        + [
            pltpu.VMEM((STAGE, 16, channels), F32),
            pltpu.VMEM((48, 10 * LANES), BF16),
            pltpu.VMEM((STAGE, channels, channels), F32),
            pltpu.VMEM((STAGE, channels, plan.depth), BF16),
            pltpu.VMEM((2, channels, 10 * LANES), F32),
            pltpu.VMEM((2, plan.depth, LANES * (reach - 2)), BF16),
            pltpu.SemaphoreType.DMA((1,)),
            pltpu.SemaphoreType.DMA((reach,)),
            pltpu.SemaphoreType.DMA((STAGE,)),
            pltpu.SemaphoreType.DMA((3 * STAGE,)),
        ],
        compiler_params=pltpu.CompilerParams(vmem_limit_bytes=56 * 2**20),
    )(*inputs, weights, kern)


def wave_kernel(plan, start, stop, pieces, base, keep_from, ending, *refs):
    levels = stop - start
    refs = list(refs)
    fresh = [refs.pop(0) for _ in pieces]
    behind_in = [refs.pop(0) for _ in range(levels)]
    mixes = [refs.pop(0) for _ in range(2)]
    kern_in = refs.pop(0)
    if ending:
        refs.pop(0)
        sums_in, classes_in = refs.pop(0), refs.pop(0)
    behind_out = {l: refs.pop(0) for l in range(max(start, keep_from), stop)}
    counts = row_counts(pieces, levels)
    count = counts[levels]
    if ending:
        final, scores = refs.pop(0), refs.pop(0)
    else:
        ends = [refs.pop(0) for _ in range(count // 2)]
    rows = [refs.pop(0) for _ in range(levels + 1)]
    kern, spread, behind, mix, taps, stacked, sums, classes = refs[:8]
    sem_k, sem_rows, sem_b, sem_w, sem_out = refs[8:]
    odd, has_next = plan.position()

    taps_in = pltpu.make_async_copy(kern_in.at[pl.ds(start, levels)], kern, sem_k.at[0])
    taps_in.start()
    moves = []
    at = 0
    for piece, (size, order, join) in zip(fresh, pieces):
        for k in range(size):
            if order == "mirror":
                place = jnp.where(odd, k, size - 1 - k)
            else:
                place = size - 1 - k
            moves.append(
                (join, pltpu.make_async_copy(piece.at[k], rows[join].at[at + place], sem_rows.at[at + k]))
            )
        at += size
    for join, move in moves:
        if join == 0:
            move.start()
    tails, weights = [], []
    for l in range(levels):
        tails.append(pltpu.make_async_copy(behind_in[l], behind.at[l], sem_b.at[l]))
        block = start + l
        weights.append(
            pltpu.make_async_copy(mixes[block // STAGE].at[block % STAGE], mix.at[l], sem_w.at[l])
        )
    for l in range(min(2, levels)):
        tails[l].start()
        weights[l].start()
    fill_spread(plan, odd, spread)
    for s in range(2):
        fill_ones(plan, stacked.at[s])
    taps_in.wait()
    make_taps(kern[0], spread[...], taps.at[0])
    for join, move in moves:
        if join > 0:
            move.start()
    for join, move in moves:
        if join == 0:
            move.wait()
    if ending:
        extra = [
            pltpu.make_async_copy(sums_in, sums, sem_k.at[1]),
            pltpu.make_async_copy(classes_in, classes, sem_k.at[2]),
        ]
        for copy in extra:
            copy.start()
    leave = []

    def send(index, source, target):
        copy = pltpu.make_async_copy(source, target, sem_out.at[index])
        copy.start()
        leave.append(copy)

    for l in range(levels):
        source, target = rows[l], rows[l + 1]
        for join, move in moves:
            if join == l and l > 0:
                move.wait()
        if start + l in behind_out:
            send(l, source.at[pl.ds(counts[l] - 2, 2)], behind_out[start + l])
        tails[l].wait()
        if l + 2 < levels:
            tails[l + 2].start()
            weights[l + 2].start()

        def store(k, value, l=l, target=target):
            if base - (start + l + 1) + k >= plan.own:
                value = jnp.where(has_next, value, 0.0)
            target[k] = value

        def between(l=l):
            if l + 1 < levels:
                make_taps(kern[l + 1], spread[...], taps.at[(l + 1) % 2])
            weights[l].wait()

        run_level(
            plan, counts[l] // 2,
            lambda k, part, l=l, source=source: (
                behind[l, k, part, :] if k < 2 else source[k - 2, part, :]
            ),
            lambda k, l=l, source=source: behind[l, 1] if k == 0 else source[k - 1],
            taps.at[l % 2], mix.at[l], stacked.at[l % 2], store, between,
        )
    last = rows[levels]
    if ending:
        for k in range(count):
            u = base - stop + k
            send(levels + k, last.at[k], final.at[jnp.where(odd, u, plan.own - 1 - u)])
        for copy in extra:
            copy.wait()
        add_rows(sums, [sums[...]] + [last[k] for k in range(count)])
        score = jnp.dot(
            classes[...], sums[...], precision=lax.Precision.HIGHEST, preferred_element_type=F32
        )
        scores[...] = jnp.broadcast_to(jnp.sum(score, axis=1, keepdims=True), scores.shape)
    else:
        for p in range(count // 2):
            send(levels + p, last.at[pl.ds(2 * p, 2)], ends[p])
    for copy in leave:
        copy.wait()


def row_counts(pieces, levels):
    return [sum(size for size, _, join in pieces if join <= l) for l in range(levels + 1)]


def wave(plan, start, stop, base, keep_from, fresh, orders, joins, behind, mixes, kern, ending=None):
    channels, width = fresh[0].shape[1:]
    pieces = tuple((f.shape[0], order, join) for f, order, join in zip(fresh, orders, joins))
    levels = stop - start
    counts = row_counts(pieces, levels)
    count = counts[levels]
    pair = jax.ShapeDtypeStruct((2, channels, width), F32)
    outs = [pair] * (stop - max(start, keep_from))
    operands = [*fresh, *behind, *mixes, kern]
    specs = [HBM] * len(outs)
    aliases = {}
    if ending is not None:
        aliases = {len(operands): len(outs)}
        operands += list(ending)
        outs += [
            jax.ShapeDtypeStruct(ending[0].shape, F32), jax.ShapeDtypeStruct((8, LANES), F32)
        ]
        specs += [HBM, VMEM]
    else:
        outs += [pair] * (count // 2)
        specs += [HBM] * (count // 2)
    return pl.pallas_call(
        functools.partial(
            wave_kernel, plan, start, stop, pieces, base, keep_from, ending is not None
        ),
        out_shape=outs,
        in_specs=[HBM] * len(operands),
        out_specs=specs,
        scratch_shapes=[pltpu.VMEM((c, channels, width), F32) for c in counts]
        + [
            pltpu.VMEM((levels, 16, channels), F32),
            pltpu.VMEM((48, 10 * LANES), BF16),
            pltpu.VMEM((levels, 2, channels, width), F32),
            pltpu.VMEM((levels, channels, plan.depth), BF16),
            pltpu.VMEM((2, channels, 10 * LANES), F32),
            pltpu.VMEM((2, plan.depth, LANES * count), BF16),
            pltpu.VMEM((channels, width), F32),
            pltpu.VMEM((8, channels), F32),
            pltpu.SemaphoreType.DMA((3,)),
            pltpu.SemaphoreType.DMA((count,)),
            pltpu.SemaphoreType.DMA((levels,)),
            pltpu.SemaphoreType.DMA((levels,)),
            pltpu.SemaphoreType.DMA((levels + count,)),
        ],
        input_output_aliases=aliases,
        compiler_params=pltpu.CompilerParams(vmem_limit_bytes=56 * 2**20),
    )(*operands)


def per_device(count, slide_map, kernels, pointwise, biases, classifier):
    own, channels, width = slide_map.shape
    levels = kernels.shape[0]
    plan = Plan(own, channels, count)
    near = [(i, i ^ 1) for i in range(count)]
    far = [(i, i + 1) for i in range(1, count - 1, 2)] + [(i + 1, i) for i in range(1, count - 1, 2)]
    send = lambda rows, pairs: lax.ppermute(rows, "space", pairs)

    near0, far0 = edges(plan, slide_map)
    near0, far0 = send(near0, near), send(far0, far)
    kern = jnp.concatenate([kernels.reshape(levels, 9, channels), biases[:, None]], axis=1)
    kern = jnp.pad(kern, ((0, 0), (0, 6), (0, 0)))

    mix0, t0, t1, t2, t3, low4 = trapezoid(plan, 0, [near0, slide_map], pointwise, kern)
    far2 = send(t2, far)
    near4 = send(low4, near)
    w2, w3, mid4, high4 = wave(
        plan, 0, 4, own, 2, [far0], ["mirror"], [0], [t0, t1, t2, t3], [mix0, mix0], kern
    )
    far4 = send(mid4, far)
    mix4, t4, t5, t6, t7, features, sums = trapezoid(
        plan, 4, [near4, low4, mid4, high4], pointwise, kern
    )
    mixes = [mix0, mix4]
    classes = jnp.pad(classifier.T, ((0, 8 - classifier.shape[1]), (0, 0)))
    features, part = wave(
        plan, 2, 8, own + 4, 8, [far2, far4], ["reverse", "reverse"], [0, 2],
        [w2, w3, t4, t5, t6, t7], mixes, kern,
        (features, sums, classes),
    )
    stride = 1
    while stride < count:
        part = part + send(part, [(i, i ^ stride) for i in range(count)])
        stride *= 2
    return features, part[: classifier.shape[1], 0] * (1.0 / (own * count * width))


def solution(mesh):
    in_specs = (P(("groups", "space"), None, None), P(), P(), P(), P())
    out_specs = (P(("groups", "space"), None, None), P("groups"))
    return jax.shard_map(
        functools.partial(per_device, mesh.shape["space"]),
        mesh=mesh, in_specs=in_specs, out_specs=out_specs, check_vma=False,
    )
```
